32 devices in a mesh: head: 4 (over y, core), shard: 8 (over z, x).
Axes of the slice: x: 2, y: 2, z: 4, core: 2. Of those that a mesh axis runs over, the one named last changes fastest.
Arguments:
- layer_input: float32 [16384, 1536], P(('shard', 'head')), may hold values from -6 to 6
- cotangent: float32 [16384, 1536], P(('shard', 'head')), may hold values from -6 to 6
- weight_in: float32 [1536, 6448], P('shard'), may hold values from -0.15625 to 0.15625
- first_in: float32 [1536, 6448], P('shard'), may hold values from -24 to 24
- second_in: float32 [1536, 6448], P('shard'), may hold values from 77.0048 to 311.296
- weight_out: float32 [3072, 1536], P('shard'), may hold values from -0.109375 to 0.109375
- first_out: float32 [3072, 1536], P('shard'), may hold values from -80 to 80
- second_out: float32 [3072, 1536], P('shard'), may hold values from 861.7984 to 3440.64
- small_params: float32 [21392], P('shard'), as said below
- first_small: float32 [21392], P('shard'), may hold values from -64 to 64
- second_small: float32 [21392], P('shard'), may hold values from 8.192 to 4259.84
Outputs:
- out: float32 [16384, 1536], P(('shard', 'head'))
- d_input: float32 [16384, 1536], P(('shard', 'head'))
- new_first_in: float32 [1536, 6448], P('shard')
- new_second_in: float32 [1536, 6448], P('shard')
- new_weight_in: float32 [1536, 6448], P('shard')
- new_first_out: float32 [3072, 1536], P('shard')
- new_second_out: float32 [3072, 1536], P('shard')
- new_weight_out: float32 [3072, 1536], P('shard')
- new_first_small: float32 [21392], P('shard')
- new_second_small: float32 [21392], P('shard')
- new_small: float32 [21392], P('shard')
The draws below stay inside these ranges and needn't reach their ends.
Inputs may be any that keep to these rules, and one draw needn't show every extreme that they name: `small_params`: packed as stated; every step offset lies in [-10, -3].
All inputs are finite; a program needn't handle non-finite values.
Results may differ from the reference program's by a relative error of at most 0.0019.
The reference program's roundings to bfloat16 on the way count: a program that leaves them out, or rounds other values in their place, can miss the bound.
Values may be sent and summed in bfloat16 or wider, within the bound.
A program may use at most 320 MiB of HBM per device.

```python
import math
import jax
import jax.numpy as jnp
from jax import lax

D = 1536
DI = 3072
HEADS = 48
HEADDIM = 64
NSTATE = 128
CONV = 4
BLOCK = 256
SEQS = 1
STEP = 5
TOKENS = 16384
LENGTH = 16384
XBC = 3328
DPROJ = 6448
SMALLV = 21392


GRAD_FACTORS = (0.3, 0.3, 0.1, 0.3, 1.1, 0.7, 0.6)


def segment_scales(factors):
    extents = [CONV * XBC, XBC, HEADS, HEADS, HEADS, DI, D]
    return jnp.concatenate([jnp.full((extent,), factor, jnp.float32) for extent, factor in zip(extents, factors)])


def draw_small_params(key, part):
    key = jax.random.fold_in(key, 11)
    conv_weight = jax.random.uniform(jax.random.fold_in(key, 1), (CONV * XBC,), jnp.float32, -0.5, 0.5)
    conv_bias = jax.random.uniform(jax.random.fold_in(key, 2), (XBC,), jnp.float32, -0.5, 0.5)
    fast_count = HEADS // 2
    ranking = jax.random.permutation(jax.random.fold_in(key, 3), HEADS)
    fast = ranking < fast_count
    slow_center = -0.5 * math.log(LENGTH * NSTATE)
    slow_offset = slow_center + jax.random.uniform(jax.random.fold_in(key, 4), (HEADS,), jnp.float32, -0.4, 0.4)
    fast_offset = jax.random.uniform(jax.random.fold_in(key, 5), (HEADS,), jnp.float32, -5.0, -4.0)
    dt_bias = jnp.where(fast, fast_offset, slow_offset)
    jitter = jax.random.uniform(jax.random.fold_in(key, 6), (HEADS,), jnp.float32, -0.3, 0.3)
    slow_alog = math.log(0.9) + 0.5 * math.log(NSTATE / LENGTH)
    a_log = jnp.where(fast, 0.33, slow_alog) + jitter
    skip_gain = jax.random.uniform(jax.random.fold_in(key, 7), (HEADS,), jnp.float32, 0.5, 1.5)
    norm_gain = jax.random.uniform(jax.random.fold_in(key, 8), (DI,), jnp.float32, 0.6, 1.4)
    pre_gain = jax.random.uniform(jax.random.fold_in(key, 9), (D,), jnp.float32, 0.6, 1.4)
    return jnp.concatenate([conv_weight, conv_bias, dt_bias, a_log, skip_gain, norm_gain, pre_gain])


def draw_first_small(key, part):
    key = jax.random.fold_in(key, 23)
    values = jax.random.truncated_normal(key, -4.0, 4.0, (SMALLV,), jnp.float32)
    return values * (0.111 * math.sqrt(TOKENS)) * segment_scales(GRAD_FACTORS)


def draw_second_small(key, part):
    key = jax.random.fold_in(key, 37)
    spread = jnp.exp(jax.random.uniform(key, (SMALLV,), jnp.float32, 0.0, math.log(4.0)))
    scales = segment_scales(GRAD_FACTORS)
    return spread * (0.0526 * TOKENS) * scales * scales


def steps_of(stream_key, dims, cuts, least, largest):
    gain, own = 1.0, jax.random.fold_in(stream_key, 6)
    for dim, parts in cuts:
        steps = jnp.exp(jax.random.uniform(jax.random.fold_in(own, dim), (parts,), jnp.float32, least / len(cuts), largest / len(cuts)))
        gain = gain * jnp.repeat(steps, dims[dim] // parts).reshape([-1 if axis == dim else 1 for axis in range(len(dims))])
    return gain


def normal_values(key, shape, scale, bound, split=(), kind=jnp.bfloat16):
    gain = steps_of(key, shape, split, -0.22, 0.18) if split else 1.0
    drawn = jax.random.normal(key, shape, jnp.float32) * scale * gain
    return jnp.minimum(jnp.maximum(drawn, -bound), bound).astype(kind)


def setup_inputs(seed: int = 0) -> dict:
    arg_keys = jax.random.split(jax.random.key(seed), 12)
    return {
        "layer_input": normal_values(arg_keys[0], (TOKENS, D), 1.0, 6.0, ((0, 32),), jnp.float32),
        "cotangent": normal_values(arg_keys[1], (TOKENS, D), 1.0, 6.0, ((0, 32),), jnp.float32),
        "weight_in": normal_values(arg_keys[2], (D, DPROJ), D ** -0.5, 0.15625, ((0, 8),), jnp.float32),
        "first_in": normal_values(arg_keys[3], (D, DPROJ), (0.033 * TOKENS ** 0.5), 24.0, ((0, 8),), jnp.float32),
        "second_in": jnp.clip(jnp.exp(math.log(311.296) - 1.3968765 * jax.random.uniform(arg_keys[4], (D, DPROJ), jnp.float32) ** steps_of(arg_keys[4], (D, DPROJ), ((0, 8),), -0.2, 0.2)), 77.0048, 311.296),
        "weight_out": normal_values(arg_keys[5], (DI, D), DI ** -0.5, 0.109375, ((0, 8),), jnp.float32),
        "first_out": normal_values(arg_keys[6], (DI, D), (0.111 * TOKENS ** 0.5), 80.0, ((0, 8),), jnp.float32),
        "second_out": jnp.clip(jnp.exp(math.log(3440.64) - 1.3843914 * jax.random.uniform(arg_keys[7], (DI, D), jnp.float32) ** steps_of(arg_keys[7], (DI, D), ((0, 8),), -0.2, 0.2)), 861.7984, 3440.64),
        "small_params": draw_small_params(jax.random.fold_in(arg_keys[11], 71), 0),
        "first_small": draw_first_small(jax.random.fold_in(arg_keys[11], 71), 0),
        "second_small": draw_second_small(jax.random.fold_in(arg_keys[11], 71), 0),
    }


@jax.custom_vjp
def low(v):
    return lax.optimization_barrier(v.astype(jnp.bfloat16)).astype(jnp.float32)

@jax.custom_vjp
def low_back(v):
    return v

def low_keep(v):
    return (low(v), None)

def low_pass(kept, grad):
    return (grad,)

def back_keep(v):
    return (v, None)

def back_low(kept, grad):
    return (low(grad),)
low.defvjp(low_keep, low_pass)
low_back.defvjp(back_keep, back_low)
EPSILON = 1e-05
BETA_FIRST = 0.9
BETA_SECOND = 0.95
ADAM_EPSILON = 1e-08
RATE_MATRIX = 0.02
RATE_SMALL = 0.2
DECAY_MATRIX = 0.1
HIGHEST = lax.Precision.HIGHEST

def unpack(packed):
    offset = 0
    conv_weight = packed[offset:offset + CONV * XBC].reshape(CONV, XBC)
    offset = offset + CONV * XBC
    conv_bias = packed[offset:offset + XBC]
    offset = offset + XBC
    dt_bias = packed[offset:offset + HEADS]
    a_log = packed[offset + HEADS:offset + 2 * HEADS]
    skip_gain = packed[offset + 2 * HEADS:offset + 3 * HEADS]
    offset = offset + 3 * HEADS
    norm_gain = packed[offset:offset + DI]
    pre_gain = packed[offset + DI:offset + DI + D]
    return (conv_weight, conv_bias, dt_bias, a_log, skip_gain, norm_gain, pre_gain)

def block_step(state, pieces):
    x_block, b_block, c_block, step_block, decay_block = pieces
    log_decay = jnp.cumsum(decay_block, axis=0)
    block_total = log_decay[-1]
    causal = jnp.arange(BLOCK)[:, None] >= jnp.arange(BLOCK)[None, :]
    spread = log_decay.T[:, :, None] - log_decay.T[:, None, :]
    weight = jnp.exp(jnp.where(causal[None], spread, -jnp.inf))
    scores = jnp.dot(c_block, b_block.T, precision=HIGHEST)
    mixing = weight * scores[None] * step_block.T[:, None, :]
    y_diag = jnp.einsum('hts,shp->thp', mixing, x_block, precision=HIGHEST)
    y_off = jnp.einsum('hpn,tn->thp', state, c_block, precision=HIGHEST) * jnp.exp(log_decay)[:, :, None]
    tail_weight = jnp.exp(block_total[None] - log_decay) * step_block
    new_state = jnp.exp(block_total)[:, None, None] * state + jnp.einsum('shp,sn->hpn', x_block * tail_weight[:, :, None], b_block, precision=HIGHEST)
    return (new_state, y_diag + y_off)

def scan_sequence(x_heads, b_rows, c_rows, step_size, decay_rows):
    block_count = LENGTH // BLOCK
    pieces = (x_heads.reshape(block_count, BLOCK, HEADS, HEADDIM), b_rows.reshape(block_count, BLOCK, NSTATE), c_rows.reshape(block_count, BLOCK, NSTATE), step_size.reshape(block_count, BLOCK, HEADS), decay_rows.reshape(block_count, BLOCK, HEADS))
    initial = jnp.zeros((HEADS, HEADDIM, NSTATE), jnp.float32)
    final_state, outputs = lax.scan(jax.checkpoint(block_step), initial, pieces)
    return outputs.reshape(LENGTH, HEADS, HEADDIM)

def forward(layer_input, weight_in, weight_out, small_params):
    weight_in = low(weight_in)
    weight_out = low(weight_out)
    conv_weight, conv_bias, dt_bias, a_log, skip_gain, norm_gain, pre_gain = unpack(low(small_params))
    inv_scale = lax.rsqrt(lax.optimization_barrier(jnp.mean(layer_input * layer_input, axis=-1, keepdims=True)) + EPSILON)
    normed = low(layer_input * inv_scale * pre_gain)
    projected = low_back(low(jnp.dot(normed, weight_in, precision=HIGHEST)))
    gate_raw = projected[:, :DI]
    xbc_raw = projected[:, DI:DI + XBC].reshape(SEQS, LENGTH, XBC)
    dt_raw = projected[:, DI + XBC:].reshape(SEQS, LENGTH, HEADS)
    padded = jnp.pad(xbc_raw, ((0, 0), (CONV - 1, 0), (0, 0)))
    conv_out = conv_bias + sum((conv_weight[tap] * padded[:, tap:tap + LENGTH] for tap in range(CONV)))
    activated = jax.nn.silu(conv_out)
    x_heads = activated[..., :DI].reshape(SEQS, LENGTH, HEADS, HEADDIM)
    b_rows = activated[..., DI:DI + NSTATE]
    c_rows = activated[..., DI + NSTATE:]
    step_size = jax.nn.softplus(dt_raw + dt_bias)
    decay_rows = step_size * -jnp.exp(a_log)
    y_ssm = jax.vmap(scan_sequence)(x_heads, b_rows, c_rows, step_size, decay_rows)
    y_mix = low((y_ssm + skip_gain[:, None] * x_heads).reshape(TOKENS, DI))
    gated = y_mix * jax.nn.silu(gate_raw)
    gate_scale = lax.rsqrt(lax.optimization_barrier(jnp.mean(gated * gated, axis=-1, keepdims=True)) + EPSILON)
    mixed = low(gated * gate_scale * norm_gain)
    return layer_input + low_back(jnp.dot(mixed, weight_out, precision=HIGHEST))

def adamw(weight, moment_one, moment_two, gradient, step_rate, weight_decay):
    moment_one = BETA_FIRST * moment_one + (1.0 - BETA_FIRST) * gradient
    moment_two = BETA_SECOND * moment_two + (1.0 - BETA_SECOND) * gradient * gradient
    first_hat = moment_one / (1.0 - BETA_FIRST ** STEP)
    second_hat = moment_two / (1.0 - BETA_SECOND ** STEP)
    weight = weight - step_rate * (first_hat / (jnp.sqrt(second_hat) + ADAM_EPSILON) + weight_decay * weight)
    return (moment_one, moment_two, weight)

def reference(layer_input, cotangent, weight_in, first_in, second_in, weight_out, first_out, second_out, small_params, first_small, second_small):
    result, pullback = jax.vjp(forward, layer_input, weight_in, weight_out, small_params)
    d_input, grad_in, grad_out, grad_small = pullback(cotangent)
    one_in, two_in, new_in = adamw(weight_in, first_in, second_in, grad_in, RATE_MATRIX, DECAY_MATRIX)
    one_out, two_out, new_out = adamw(weight_out, first_out, second_out, grad_out, RATE_MATRIX, DECAY_MATRIX)
    one_small, two_small, new_small = adamw(small_params, first_small, second_small, grad_small, RATE_SMALL, 0.0)
    return (result, d_input, one_in, two_in, new_in, one_out, two_out, new_out, one_small, two_small, new_small)
```

```python
import functools

import jax
import jax.numpy as jnp
from jax import lax
from jax.experimental import pallas as pl
from jax.experimental.pallas import tpu as pltpu
from jax.sharding import PartitionSpec as P

D = 1536
DI = 3072
HEADS = 48
HEADDIM = 64
NSTATE = 128
CONV = 4
BLOCK = 256
STEP = 5
XBC = 3328
HALO = 16
LANES = 128


EPSILON = 1e-05
BETA_FIRST = 0.9
BETA_SECOND = 0.95
ADAM_EPSILON = 1e-08
RATE_MATRIX = 0.02
RATE_SMALL = 0.2
DECAY_MATRIX = 0.1
F32 = jnp.float32
BF16 = jnp.bfloat16


def unpack(packed):
    offset = 0
    conv_weight = packed[offset : offset + CONV * XBC].reshape(CONV, XBC)
    offset = offset + CONV * XBC
    conv_bias = packed[offset : offset + XBC]
    offset = offset + XBC
    dt_bias = packed[offset : offset + HEADS]
    a_log = packed[offset + HEADS : offset + 2 * HEADS]
    skip_gain = packed[offset + 2 * HEADS : offset + 3 * HEADS]
    offset = offset + 3 * HEADS
    norm_gain = packed[offset : offset + DI]
    pre_gain = packed[offset + DI : offset + DI + D]
    return (conv_weight, conv_bias, dt_bias, a_log, skip_gain, norm_gain, pre_gain)


def adamw(weight, moment_one, moment_two, gradient, step_rate, weight_decay):
    moment_one = BETA_FIRST * moment_one + (1.0 - BETA_FIRST) * gradient
    moment_two = BETA_SECOND * moment_two + (1.0 - BETA_SECOND) * gradient * gradient
    first_hat = moment_one / (1.0 - BETA_FIRST**STEP)
    second_hat = moment_two / (1.0 - BETA_SECOND**STEP)
    weight = weight - step_rate * (
        first_hat / (jnp.sqrt(second_hat) + ADAM_EPSILON) + weight_decay * weight
    )
    return (moment_one, moment_two, weight)


def swap_core(value):
    peers = lax.axis_size("head")
    return lax.ppermute(value, "head", [(i, i ^ 1) for i in range(peers)])


def shift_chip(value, by):
    peers = lax.axis_size("head")
    chips = peers // 2
    return lax.ppermute(
        value, "head", [(i, ((i // 2 + by) % chips) * 2 + i % 2) for i in range(peers)]
    )


def gather_head(value):
    peers = lax.axis_size("head")
    chips = peers // 2
    mine = lax.axis_index("head")
    chip, core = mine // 2, mine % 2
    rows = value.shape[0]
    pieces = [(mine, value)]
    for by in range(1, chips):
        far = shift_chip(value, by)
        source = lax.rem(chip + chips - by, chips) * 2 + core
        pieces.append((source, far))
        pieces.append((lax.bitwise_xor(source, 1), swap_core(far)))
    pieces.append((lax.bitwise_xor(mine, 1), swap_core(value)))
    whole = jnp.zeros((peers * rows,) + value.shape[1:], value.dtype)
    for source, piece in pieces:
        whole = lax.dynamic_update_slice_in_dim(whole, piece, source * rows, 0)
    return whole


def sum_head(value):
    chips = lax.axis_size("head") // 2
    total = value
    for by in range(1, chips):
        total = total + shift_chip(value, by)
    return total + swap_core(total)


def shift_shard(value, by):
    peers = lax.axis_size("shard")
    pairs = [(i, i + by) for i in range(peers) if 0 <= i + by < peers]
    return lax.ppermute(value, "shard", pairs)


def split(value):
    high = value.astype(BF16)
    return high, (value - high.astype(F32)).astype(BF16)


def contract(a, b, dims):
    return lax.dot_general(a, b, (dims, ((), ())), preferred_element_type=F32)


NN = ((1,), (0,))
NT = ((1,), (1,))


def dot3(a, b, dims):
    (ah, al), (bh, bl) = a, b
    return contract(ah, bh, dims) + (contract(ah, bl, dims) + contract(al, bh, dims))


def running(value, forward):
    rows = value.shape[0]
    here = lax.broadcasted_iota(jnp.int32, (rows, rows), 0)
    other = lax.broadcasted_iota(jnp.int32, (rows, rows), 1)
    mask = jnp.where(here >= other if forward else here <= other, 1.0, 0.0).astype(BF16)
    high, mid = split(value)
    low = ((value - high.astype(F32)) - mid.astype(F32)).astype(BF16)
    return contract(mask, high, NN) + (contract(mask, mid, NN) + contract(mask, low, NN))


def spread_heads(value, base, width):
    rows = value.shape[0]
    left = lax.broadcasted_iota(jnp.int32, (rows, LANES), 1) < HEADDIM
    tiles = []
    for pair in range(width // LANES):
        lane = base + 2 * pair
        tiles.append(
            jnp.where(
                left,
                jnp.broadcast_to(value[:, lane : lane + 1], (rows, LANES)),
                jnp.broadcast_to(value[:, lane + 1 : lane + 2], (rows, LANES)),
            )
        )
    return jnp.concatenate(tiles, axis=1)


def gather_heads(value, base):
    width = value.shape[1]
    channel = lax.broadcasted_iota(jnp.int32, (width, LANES), 0)
    lane = lax.broadcasted_iota(jnp.int32, (width, LANES), 1)
    chosen = (channel >= (lane - base) * HEADDIM) & (channel < (lane - base + 1) * HEADDIM)
    mask = jnp.where(chosen, 1.0, 0.0).astype(BF16)
    high, low = split(value)
    return contract(high, mask, NN) + contract(low, mask, NN)


def half_masks(rows):
    lane = lax.broadcasted_iota(jnp.int32, (rows, LANES), 1)
    return lane < HEADDIM, lane >= HEADDIM


def pair_product(mats, value):
    high, low = split(value)
    zero = jnp.zeros_like(high)
    parts = []
    for mat, keep in zip(mats, half_masks(value.shape[0])):
        mh, ml = split(mat)
        vh = jnp.where(keep, high, zero)
        both = jnp.concatenate([vh, jnp.where(keep, low, zero)], axis=1)
        wide = contract(mh, both, NN)
        parts.append(wide[:, :LANES] + (wide[:, LANES:] + contract(ml, vh, NN)))
    return parts[0] + parts[1]


def prepare_kernel(
    base, x_ref, b_ref, c_ref, misc_ref, hx_ref, hb_ref, hc_ref, taps_ref, heads_ref,
    act_ref, der_ref, time_ref, state_ref, decay_ref, rows_ref, total_ref,
):
    step = pl.program_id(0)
    width = x_ref.shape[1]

    @pl.when(step == 0)
    def _():
        rows_ref[0:8, 0:width] = hx_ref[...].astype(F32)[8:16]
        rows_ref[0:8, width : width + NSTATE] = hb_ref[...].astype(F32)[8:16]
        rows_ref[0:8, width + NSTATE :] = hc_ref[...].astype(F32)[8:16]
        state_ref[...] = jnp.zeros_like(state_ref)
        total_ref[...] = jnp.zeros_like(total_ref)

    rows_ref[8:, 0:width] = x_ref[...].astype(F32)
    rows_ref[8:, width : width + NSTATE] = b_ref[...].astype(F32)
    rows_ref[8:, width + NSTATE :] = c_ref[...].astype(F32)
    for start in range(0, width + 2 * NSTATE, LANES):
        cols = slice(start, start + LANES)
        conv = taps_ref[CONV : CONV + 1, cols]
        for tap in range(CONV):
            first = 8 - (CONV - 1) + tap
            conv = conv + taps_ref[tap : tap + 1, cols] * rows_ref[first : first + BLOCK, cols]
        sig = jax.nn.sigmoid(conv)
        act_ref[:, cols] = conv * sig
        der_ref[:, cols] = sig * (1.0 + conv * (1.0 - sig))
    rows_ref[0:8, :] = rows_ref[BLOCK : BLOCK + 8, :]

    size = jax.nn.softplus(misc_ref[...].astype(F32) + heads_ref[0:1, :])
    log_decay = running(size * heads_ref[1:2, :], True)
    time_ref[:, :LANES] = size
    time_ref[:, LANES:] = log_decay
    last = log_decay[BLOCK - 1 : BLOCK, :]
    weighted = act_ref[:, 0:width] * spread_heads(jnp.exp(last - log_decay) * size, base, width)
    b_turned = jnp.transpose(act_ref[:, width : width + NSTATE])
    state_ref[...] = state_ref[...] * spread_heads(jnp.exp(last), base, width) + dot3(
        split(b_turned), split(weighted), NN
    )
    total_ref[...] = total_ref[...] + jnp.broadcast_to(last, total_ref.shape)
    decay_ref[...] = spread_heads(jnp.exp(total_ref[...]), base, width)


def forward_kernel(
    base, act_ref, time_ref, gate_ref, dmix_ref, chan_ref, prior_ref,
    ymix_ref, yssm_ref, sums_ref, before_ref, final_ref,
):
    step = pl.program_id(0)
    width = gate_ref.shape[1]

    @pl.when(step == 0)
    def _():
        final_ref[...] = prior_ref[...]

    state = final_ref[...]
    before_ref[...] = state
    size, log_decay = time_ref[:, :LANES], time_ref[:, LANES:]
    decay_rows = jnp.transpose(log_decay)
    last = log_decay[BLOCK - 1 : BLOCK, :]
    b_act, c_act = act_ref[:, width : width + NSTATE], act_ref[:, width + NSTATE :]
    c_parts = split(c_act)
    here = lax.broadcasted_iota(jnp.int32, (BLOCK, BLOCK), 0)
    other = lax.broadcasted_iota(jnp.int32, (BLOCK, BLOCK), 1)
    causal = here >= other
    scores = dot3(c_parts, split(b_act), NT)
    reach = jnp.exp(log_decay)
    carried = dot3(c_parts, split(state), NN)
    square = jnp.zeros((BLOCK, 1), F32)
    cross = jnp.zeros((BLOCK, 1), F32)
    for pair in range(width // LANES):
        cols = slice(pair * LANES, (pair + 1) * LANES)
        lane = base + 2 * pair
        x_pair = act_ref[:, cols]
        scaled = x_pair * spread_heads(size[:, lane : lane + 2], 0, LANES)
        mats = []
        for q in range(2):
            gap = log_decay[:, lane + q : lane + q + 1] - decay_rows[lane + q : lane + q + 1, :]
            mats.append(jnp.exp(jnp.where(causal, gap, -jnp.inf)) * scores)
        y_ssm = pair_product(mats, scaled) + carried[:, cols] * spread_heads(
            reach[:, lane : lane + 2], 0, LANES
        )
        yssm_ref[:, cols] = y_ssm
        y_mix = (y_ssm + chan_ref[0:1, cols] * x_pair).astype(BF16)
        ymix_ref[:, cols] = y_mix
        gate = gate_ref[:, cols].astype(F32)
        gated = y_mix.astype(F32) * (gate * jax.nn.sigmoid(gate))
        square = square + jnp.sum(gated * gated, axis=1, keepdims=True)
        cross = cross + jnp.sum(
            dmix_ref[:, cols] * chan_ref[1:2, cols] * gated, axis=1, keepdims=True
        )
    lane_id = lax.broadcasted_iota(jnp.int32, (BLOCK, LANES), 1)
    both = jnp.where(lane_id == 0, square, jnp.where(lane_id == 1, cross, 0.0))
    sums_ref[...] = jnp.transpose(both)[0:8, :]
    weighted = act_ref[:, 0:width] * spread_heads(jnp.exp(last - log_decay) * size, base, width)
    final_ref[...] = state * spread_heads(jnp.exp(last), base, width) + dot3(
        split(jnp.transpose(b_act)), split(weighted), NN
    )


def gate_kernel(
    base, c_ref, time_ref, gate_ref, dmix_ref, ymix_ref, sums_ref, chan_ref,
    mixed_ref, dgate_ref, dy_ref, state_ref, gain_ref,
):
    step = pl.program_id(0)
    width = gate_ref.shape[1]

    @pl.when(step == 0)
    def _():
        state_ref[...] = jnp.zeros_like(state_ref)
        gain_ref[...] = jnp.zeros_like(gain_ref)

    sums = jnp.transpose(jnp.concatenate([sums_ref[...]] * (LANES // 8), axis=0))
    scale = lax.rsqrt(sums[:, 0:1] / DI + EPSILON)
    unit_mean = scale * (sums[:, 1:2] / DI)
    log_decay = time_ref[...]
    last = log_decay[BLOCK - 1 : BLOCK, :]
    reach = jnp.exp(log_decay)
    c_turned = split(jnp.transpose(c_ref[...]))
    for pair in range(width // LANES):
        cols = slice(pair * LANES, (pair + 1) * LANES)
        lane = base + 2 * pair
        gate = gate_ref[:, cols].astype(F32)
        sig = jax.nn.sigmoid(gate)
        silu = gate * sig
        y_mix = ymix_ref[:, cols].astype(F32)
        d_mixed = dmix_ref[:, cols]
        gain = chan_ref[1:2, cols]
        unit = y_mix * silu * scale
        mixed_ref[:, cols] = (unit * gain).astype(BF16)
        gain_ref[:, cols] = gain_ref[:, cols] + jnp.sum(d_mixed * unit, axis=0, keepdims=True)
        d_gated = scale * (d_mixed * gain - unit * unit_mean)
        d_y = d_gated * silu
        dy_ref[:, cols] = d_y
        dgate_ref[:, cols] = (d_gated * y_mix * sig * (1.0 + gate * (1.0 - sig))).astype(BF16)
        scaled = d_y * spread_heads(reach[:, lane : lane + 2], 0, LANES)
        state_ref[:, cols] = state_ref[:, cols] * spread_heads(
            jnp.exp(last[:, lane : lane + 2]), 0, LANES
        ) + dot3(c_turned, split(scaled), NN)


def backward_kernel(
    base, local_heads, act_ref, der_ref, time_ref, dy_ref, yssm_ref, before_ref, final_ref, after_ref,
    misc_ref, x_ref, b_ref, c_ref, px_ref, pb_ref, pc_ref, hx_ref, hb_ref, hc_ref,
    taps_ref, heads_ref, chan_ref,
    drest_ref, dbc_ref, first_ref, rest_ref, gtap_ref, gskip_ref, ghead_ref,
    state_ref, tail_ref, next_ref, rows_ref, dact_ref,
):
    step = pl.program_id(0)
    steps = pl.num_programs(0)
    width = dy_ref.shape[1]

    @pl.when(step == 0)
    def _():
        state_ref[...] = after_ref[...]
        product = after_ref[...] * final_ref[...]
        tail = jnp.sum(gather_heads(product, base), axis=0, keepdims=True)
        tail_ref[...] = jnp.broadcast_to(tail, tail_ref.shape)
        next_ref[BLOCK:, :] = jnp.zeros((8, width + 2 * NSTATE), F32)
        gtap_ref[...] = jnp.zeros_like(gtap_ref)
        gskip_ref[...] = jnp.zeros_like(gskip_ref)
        ghead_ref[...] = jnp.zeros_like(ghead_ref)

    state = state_ref[...]
    size, log_decay = time_ref[:, :LANES], time_ref[:, LANES:]
    decay_rows = jnp.transpose(log_decay)
    last = log_decay[BLOCK - 1 : BLOCK, :]
    b_act, c_act = act_ref[:, width : width + NSTATE], act_ref[:, width + NSTATE :]
    b_parts, c_parts = split(b_act), split(c_act)
    here = lax.broadcasted_iota(jnp.int32, (BLOCK, BLOCK), 0)
    other = lax.broadcasted_iota(jnp.int32, (BLOCK, BLOCK), 1)
    causal = other >= here
    scores = dot3(b_parts, c_parts, NT)
    reach = jnp.exp(log_decay)
    to_end = jnp.exp(last - log_decay)
    state_parts = split(state)
    carried = dot3(b_parts, state_parts, NN)
    masks = half_masks(BLOCK)
    pairs = jnp.zeros((BLOCK, BLOCK), F32)
    along = jnp.zeros((BLOCK, LANES), F32)
    for pair in range(width // LANES):
        cols = slice(pair * LANES, (pair + 1) * LANES)
        lane = base + 2 * pair
        x_pair, dy_pair = act_ref[:, cols], dy_ref[:, cols]
        size_pair = spread_heads(size[:, lane : lane + 2], 0, LANES)
        xs_high, xs_low = split(x_pair * size_pair)
        dy_high, dy_low = split(dy_pair)
        zero = jnp.zeros_like(xs_high)
        mats = []
        for q in range(2):
            gap = decay_rows[lane + q : lane + q + 1, :] - log_decay[:, lane + q : lane + q + 1]
            weight = jnp.exp(jnp.where(causal, gap, -jnp.inf))
            mats.append(weight * scores)
            xh = jnp.where(masks[q], xs_high, zero)
            xl = jnp.where(masks[q], xs_low, zero)
            found = contract(
                jnp.concatenate([xh, xl], axis=1), jnp.concatenate([dy_high, dy_high], axis=1), NT
            ) + contract(xh, dy_low, NT)
            pairs = pairs + found * weight
        q_all = pair_product(mats, dy_pair) + carried[:, cols] * spread_heads(
            to_end[:, lane : lane + 2], 0, LANES
        )
        dx = q_all * size_pair + chan_ref[0:1, cols] * dy_pair
        next_ref[0:BLOCK, cols] = dx * der_ref[:, cols]
        gskip_ref[:, cols] = gskip_ref[:, cols] + jnp.sum(dy_pair * x_pair, axis=0, keepdims=True)
        dact_ref[:, cols] = x_pair * q_all
    pairs_parts = split(pairs)
    turned_parts = split(jnp.transpose(pairs))
    weighted = act_ref[:, 0:width] * spread_heads(to_end * size, base, width)
    d_b = dot3(pairs_parts, c_parts, NN) + dot3(split(weighted), state_parts, NT)
    scaled = split(dy_ref[...] * spread_heads(reach, base, width))
    d_c = dot3(turned_parts, b_parts, NN) + dot3(scaled, split(before_ref[...]), NT)
    next_ref[0:BLOCK, width : width + NSTATE] = d_b * der_ref[:, width : width + NSTATE]
    next_ref[0:BLOCK, width + NSTATE :] = d_c * der_ref[:, width + NSTATE :]
    state_ref[...] = state * spread_heads(jnp.exp(last), base, width) + dot3(
        split(jnp.transpose(c_act)), scaled, NN
    )

    along = gather_heads(dy_ref[...] * yssm_ref[...], base)
    across = gather_heads(dact_ref[...], base)
    d_log = running(along - size * across, False) + tail_ref[0:1, :]
    tail_ref[...] = jnp.broadcast_to(d_log[0:1, :], tail_ref.shape)
    lane_id = lax.broadcasted_iota(jnp.int32, (BLOCK, LANES), 1)
    mine = (lane_id >= base) & (lane_id < base + local_heads)
    d_size = across + d_log * heads_ref[1:2, :]
    d_dt = jnp.where(
        mine, d_size * jax.nn.sigmoid(misc_ref[...].astype(F32) + heads_ref[0:1, :]), 0.0
    )
    drest_ref[:, width:] = d_dt.astype(BF16)
    ghead_ref[0:1, :] = ghead_ref[0:1, :] + jnp.sum(d_dt, axis=0, keepdims=True)
    ghead_ref[1:2, :] = ghead_ref[1:2, :] + jnp.sum(d_log * size, axis=0, keepdims=True)

    begin = step == steps - 1
    for kept, first, start in (
        (px_ref, hx_ref, slice(0, width)),
        (pb_ref, hb_ref, slice(width, width + NSTATE)),
        (pc_ref, hc_ref, slice(width + NSTATE, width + 2 * NSTATE)),
    ):
        rows_ref[0:8, start] = jnp.where(begin, first[...].astype(F32)[8:16], kept[...].astype(F32)[8:16])
    rows_ref[8:, 0:width] = x_ref[...].astype(F32)
    rows_ref[8:, width : width + NSTATE] = b_ref[...].astype(F32)
    rows_ref[8:, width + NSTATE :] = c_ref[...].astype(F32)
    for start in range(0, width + 2 * NSTATE, LANES):
        cols = slice(start, start + LANES)
        d_conv = next_ref[0:BLOCK, cols]
        d_raw = jnp.zeros((BLOCK, LANES), F32)
        for tap in range(CONV):
            ahead = CONV - 1 - tap
            d_raw = d_raw + taps_ref[tap : tap + 1, cols] * next_ref[ahead : ahead + BLOCK, cols]
            first = 8 - (CONV - 1) + tap
            gtap_ref[tap : tap + 1, cols] = gtap_ref[tap : tap + 1, cols] + jnp.sum(
                d_conv * rows_ref[first : first + BLOCK, cols], axis=0, keepdims=True
            )
        gtap_ref[CONV : CONV + 1, cols] = gtap_ref[CONV : CONV + 1, cols] + jnp.sum(
            d_conv, axis=0, keepdims=True
        )
        if start < width:
            drest_ref[:, cols] = d_raw.astype(BF16)
        else:
            dbc_ref[start - width : start - width + LANES, :] = jnp.transpose(d_raw)

        @pl.when(step == 0)
        def _():
            rest_ref[:, cols] = d_raw[BLOCK - 16 :]

    next_ref[BLOCK:, :] = next_ref[0:8, :]
    first_ref[...] = next_ref[0:8, :]


def chain_kernel(direction, own_ref, decay_ref, prior_ref, inbox, outbox, send_sems, recv_sems):
    peers = lax.axis_size("shard")
    mine = lax.axis_index("shard")
    has_source = mine > 0 if direction > 0 else mine < peers - 1
    has_target = mine < peers - 1 if direction > 0 else mine > 0
    source, target = mine - direction, mine + direction
    barrier = pltpu.get_barrier_semaphore()

    @pl.when(has_source)
    def _():
        pl.semaphore_signal(
            barrier, inc=1, device_id={"shard": source}, device_id_type=pl.DeviceIdType.MESH
        )

    @pl.when(has_target)
    def _():
        pl.semaphore_wait(barrier, 1)

    count = send_sems.shape[0]
    rows = inbox.shape[0] // count

    def copy(piece):
        at = pl.ds(piece * rows, rows)
        return pltpu.make_async_remote_copy(
            src_ref=outbox.at[at],
            dst_ref=inbox.at[at],
            send_sem=send_sems.at[piece],
            recv_sem=recv_sems.at[piece],
            device_id={"shard": target},
            device_id_type=pl.DeviceIdType.MESH,
        )

    for piece in range(count):
        at = slice(piece * rows, (piece + 1) * rows)

        @pl.when(has_source)
        def _():
            copy(piece).wait_recv()
            prior_ref[at, :] = inbox[at, :]

        @pl.when(jnp.logical_not(has_source))
        def _():
            prior_ref[at, :] = jnp.zeros((rows, inbox.shape[1]), F32)

        @pl.when(has_target)
        def _():
            outbox[at, :] = prior_ref[at, :] * decay_ref[0:1, :] + own_ref[at, :]
            copy(piece).start()

    @pl.when(has_target)
    def _():
        for piece in range(count):
            copy(piece).wait_send()


PIECES = 8
VMEM_LIMIT = 48 * 1024 * 1024


def chain(own, decay, direction):
    shape = own.shape
    return pl.pallas_call(
        functools.partial(chain_kernel, direction),
        out_shape=jax.ShapeDtypeStruct(shape, F32),
        in_specs=[pl.BlockSpec(memory_space=pltpu.VMEM)] * 2,
        out_specs=pl.BlockSpec(memory_space=pltpu.VMEM),
        scratch_shapes=[
            pltpu.VMEM(shape, F32),
            pltpu.VMEM(shape, F32),
            pltpu.SemaphoreType.DMA((PIECES,)),
            pltpu.SemaphoreType.DMA((PIECES,)),
        ],
        compiler_params=pltpu.CompilerParams(
            collective_id=1,
            has_side_effects=True,
            vmem_limit_bytes=VMEM_LIMIT,
        ),
        name="carry_forward",
    )(own, decay)


def blocked(kernel, name, steps, operands, results, scratch, flops, moved):
    return pl.pallas_call(
        kernel,
        grid=(steps,),
        in_specs=[pl.BlockSpec(block, index) for _, block, index in operands],
        out_specs=[pl.BlockSpec(block, index) for _, _, block, index in results],
        out_shape=[jax.ShapeDtypeStruct(shape, kind) for shape, kind, _, _ in results],
        scratch_shapes=scratch,
        compiler_params=pltpu.CompilerParams(
            dimension_semantics=("arbitrary",), vmem_limit_bytes=VMEM_LIMIT
        ),
        cost_estimate=pl.CostEstimate(flops=flops, bytes_accessed=moved, transcendentals=0),
        name=name,
    )(*[array for array, _, _ in operands])


RING_ROWS = 4
MESH = pl.DeviceIdType.MESH


def ring_position(shard, peers):
    across = peers // RING_ROWS
    row, col = lax.div(shard, across), lax.rem(shard, across)
    turn = RING_ROWS - 1 - row
    inner = jnp.where(lax.rem(turn, 2) == 0, col - 1, across - 1 - col)
    return jnp.where(col == 0, row, RING_ROWS + turn * (across - 1) + inner)


def ring_shard(position, peers):
    across = peers // RING_ROWS
    place = lax.rem(position + 2 * peers, peers)
    after = jnp.maximum(place - RING_ROWS, 0)
    turn, inner = lax.div(after, across - 1), lax.rem(after, across - 1)
    col = jnp.where(lax.rem(turn, 2) == 0, inner + 1, across - 1 - inner)
    back = (RING_ROWS - 1 - turn) * across + col
    return jnp.where(place < RING_ROWS, jnp.minimum(place, RING_ROWS - 1) * across, back)


def cut_rows(rows, tile):
    parts = 2 if rows % (4 * tile) == 0 else 1
    half = -(-rows // (2 * tile)) * tile
    pieces = []
    for start, length, way in ((0, half, 1), (half, rows - half, -1)):
        size = length // parts
        pieces += [(start + i * size, size, way) for i in range(parts)]
    return sorted(pieces, key=lambda piece: (piece[0] - (half if piece[2] < 0 else 0), -piece[2]))


def greet(others):
    barrier = pltpu.get_barrier_semaphore()
    for device in others:
        pl.semaphore_signal(barrier, inc=1, device_id=device, device_id_type=MESH)
    return barrier


def remote(source, target, send, recv, device):
    return pltpu.make_async_remote_copy(
        src_ref=source, dst_ref=target, send_sem=send, recv_sem=recv, device_id=device, device_id_type=MESH
    )


def head_peers():
    peers = lax.axis_size("head")
    mine = lax.axis_index("head")
    chips = peers // 2
    chip, core = lax.div(mine, 2), lax.rem(mine, 2)
    there = [lax.rem(chip + by, chips) * 2 + core for by in range(1, chips)]
    source = [lax.rem(chip + chips - by, chips) * 2 + core for by in range(1, chips)]
    return mine + 1 - 2 * core, there, source


def worker_of(head, shard, heads, peers):
    stored, worked = shard * heads + head, head * peers + shard
    target = (lax.div(stored, peers), lax.rem(stored, peers))
    origin = (lax.rem(worked, heads), lax.div(worked, heads))
    return target, origin, stored == worked


def home_of(head, shard, heads, peers):
    target, origin, at_home = worker_of(head, shard, heads, peers)
    return origin, target, at_home


def greet_across(barrier, origin, at_home, usual):
    @pl.when(jnp.logical_not(at_home))
    def _():
        pl.semaphore_signal(barrier, inc=1, device_id=origin, device_id_type=MESH)
        pl.semaphore_wait(barrier, usual + 1)

    @pl.when(at_home)
    def _():
        pl.semaphore_wait(barrier, usual)


class HeadGather:
    def __init__(self, own, whole, sems):
        peers = lax.axis_size("head")
        mine = lax.axis_index("head")
        self.sibling, self.there, self.source = head_peers()
        rows = whole.shape[0] // peers
        hint = 16 if whole.dtype == BF16 else 8
        self.at = lambda owner: whole.at[pl.ds(pl.multiple_of(owner * rows, hint), rows)]
        self.own, self.mine = own, mine
        self.far_send, self.far_recv, self.near_send, self.near_recv = sems

    def far(self, by):
        return remote(
            self.own, self.at(self.mine), self.far_send.at[by], self.far_recv.at[by], {"head": self.there[by]}
        )

    def near(self, by):
        source = self.own if by < 0 else self.at(self.source[by])
        target = self.at(self.mine) if by < 0 else self.at(self.source[by])
        return remote(
            source, target, self.near_send.at[by + 1], self.near_recv.at[by + 1], {"head": self.sibling}
        )

    def start(self):
        for by in range(len(self.there)):
            self.far(by).start()
        self.near(-1).start()

    def pass_on(self):
        for by in range(len(self.there)):
            self.far(by).wait_recv()
            self.near(by).start()

    def finish(self):
        for by in range(-1, len(self.there)):
            self.near(by).wait_recv()

    def drain(self):
        for by in range(len(self.there)):
            self.far(by).wait_send()
        for by in range(-1, len(self.there)):
            self.near(by).wait_send()


def gather_kernel(ring_out, pieces, out_pieces, small_ref, chunk_ref, input_ref, cot_ref, out_ref, *refs):
    full_ref, normed_ref, cot_full_ref, projected_ref, smalls_ref, before_ref = refs[:6]
    refs = refs[6:]
    if ring_out:
        full_out_ref, refs = refs[0], refs[1:]
    (
        full, normed, cot_own, projected, inbox, rim, small_send, small_recv, ring_send, ring_recv,
        far_send, far_recv, near_send, near_recv, cot_far_send, cot_far_recv, cot_near_send, cot_near_recv,
        rim_send, rim_recv, local_sems, tile_sems,
    ) = refs[:22]
    if ring_out:
        full_out, piece_send, piece_recv, out_send, out_recv = refs[22:]
    peers, heads = lax.axis_size("shard"), lax.axis_size("head")
    shard, head = lax.axis_index("shard"), lax.axis_index("head")
    sibling, there, _ = head_peers()
    rows, tokens = chunk_ref.shape[0], input_ref.shape[0]
    others = [lax.rem(shard + by, peers) for by in range(1, peers)]
    barrier = greet(
        [{"shard": other} for other in others]
        + [{"head": other} for other in there]
        + [{"head": sibling}]
    )
    usual = peers - 1 + len(there) + 1
    if ring_out:
        target, origin, at_home = worker_of(head, shard, heads, peers)
        greet_across(barrier, origin, at_home, usual)
    else:
        pl.semaphore_wait(barrier, usual)
    place = ring_position(shard, peers)
    following, preceding = ring_shard(place + 1, peers), ring_shard(place - 1, peers)
    small_copies = [
        remote(
            small_ref, inbox.at[by], small_send.at[by], small_recv.at[by], {"shard": others[by]}
        )
        for by in range(peers - 1)
    ]
    for copy in small_copies:
        copy.start()

    def hop(chunk, whole, cuts, sends, recvs, index, step):
        first, size, way = cuts[index]
        owner = ring_shard(place - way * step, peers)
        each = whole.shape[0] // peers
        at = whole.at[pl.ds(pl.multiple_of(owner * each + first, 16), size)]
        return remote(
            chunk.at[pl.ds(first, size)] if step == 0 and chunk is not None else at,
            at,
            sends.at[index, step],
            recvs.at[index, step],
            {"shard": following if way > 0 else preceding},
        )

    in_hop = functools.partial(hop, chunk_ref, full, pieces, ring_send, ring_recv)
    for index in range(len(pieces)):
        in_hop(index, 0).start()
    keep = pltpu.make_async_copy(
        chunk_ref, full.at[pl.ds(pl.multiple_of(shard * rows, 16), rows)], local_sems.at[0]
    )
    keep.start()

    for copy in small_copies:
        copy.wait_recv()
    smalls_ref[pl.ds(shard, 1)] = small_ref[...][None]
    gain = small_ref[SMALL_ROWS:, :].astype(F32)
    for by in range(1, peers):
        from_there = lax.rem(shard + peers - by, peers)
        smalls_ref[pl.ds(from_there, 1)] = inbox[by - 1][None]
        gain = gain + inbox[by - 1, SMALL_ROWS:, :].astype(F32)
    gain = jnp.concatenate([gain[i : i + 1, :] for i in range(D // LANES)], axis=1)
    tile = 128
    for start in range(0, tokens, tile):
        value = input_ref[pl.ds(start, tile), :]
        scale = lax.rsqrt(jnp.mean(value * value, axis=-1, keepdims=True) + EPSILON)
        at = pl.ds(pl.multiple_of(head * tokens + start, tile), tile)
        normed[at, :] = (value * scale * gain).astype(BF16)
    mine = pl.ds(pl.multiple_of(head * tokens, 16), tokens)
    normed_gather = HeadGather(normed.at[mine], normed, (far_send, far_recv, near_send, near_recv))
    normed_gather.start()
    for start in range(0, tokens, tile):
        at = pl.ds(start, tile)
        cot_own[at, :] = cot_ref[at, :].astype(BF16)
    cot_gather = HeadGather(
        cot_own, cot_full_ref, (cot_far_send, cot_far_recv, cot_near_send, cot_near_recv)
    )
    cot_stay = pltpu.make_async_copy(cot_own, cot_full_ref.at[mine], local_sems.at[1])
    cot_stay.start()

    if ring_out:
        each = out_ref.shape[0]
        piece_copy = remote(
            out_ref, full_out.at[pl.ds(pl.multiple_of(target[1] * each, 16), each)],
            piece_send, piece_recv, target,
        )

        @pl.when(at_home)
        def _():
            full_out[pl.ds(pl.multiple_of(shard * each, 16), each), :] = out_ref[...]

        @pl.when(jnp.logical_not(at_home))
        def _():
            piece_copy.start()

    for step in range(1, peers - 1):
        for index in range(len(pieces)):
            in_hop(index, step - 1).wait_recv()
            in_hop(index, step).start()
        if step == min(5, peers - 2):
            normed_gather.pass_on()
            cot_gather.start()
    for index in range(len(pieces)):
        in_hop(index, peers - 2).wait_recv()
    keep.wait()
    normed_gather.finish()
    rim_copy = remote(
        normed.at[pl.ds(heads * tokens - HALO, HALO)], rim, rim_send, rim_recv,
        {"shard": lax.rem(shard + 1, peers)},
    )
    rim_copy.start()
    out_copies = [
        pltpu.make_async_copy(full, full_ref, local_sems.at[2]),
        pltpu.make_async_copy(normed, normed_ref, local_sems.at[3]),
    ]
    for copy in out_copies:
        copy.start()

    tiles = heads * tokens // BLOCK

    def tile_copy(number):
        at = pl.ds(pl.multiple_of(number * BLOCK, BLOCK), BLOCK)
        return pltpu.make_async_copy(projected.at[at], projected_ref.at[at], tile_sems.at[number])

    def project(number, carry):
        at = pl.ds(pl.multiple_of(number * BLOCK, BLOCK), BLOCK)
        projected[at, :] = contract(normed[at, :], full[...], NN).astype(BF16)
        tile_copy(number).start()
        return carry

    if ring_out:

        @pl.when(jnp.logical_not(at_home))
        def _():
            piece_copy.wait()

        out_hop = functools.partial(hop, None, full_out, out_pieces, out_send, out_recv)
        for step in range(peers - 1):
            for index in range(len(out_pieces)):
                if step:
                    out_hop(index, step - 1).wait_recv()
                out_hop(index, step).start()
            low, high = min(step, tiles), min(step + 1, tiles) if step < peers - 2 else tiles
            if low < high:
                lax.fori_loop(low, high, project, 0)
        for index in range(len(out_pieces)):
            out_hop(index, peers - 2).wait_recv()
        out_copies.append(pltpu.make_async_copy(full_out, full_out_ref, local_sems.at[4]))
        out_copies[-1].start()
    else:
        lax.fori_loop(0, tiles, project, 0)
    cot_gather.pass_on()
    rim_copy.wait_recv()
    before = contract(rim[...], full[...], NN)
    before_ref[...] = jnp.where(shard > 0, before, 0.0).astype(BF16)

    cot_gather.finish()
    cot_gather.drain()
    normed_gather.drain()
    for copy in small_copies:
        copy.wait_send()
    for index in range(len(pieces)):
        for step in range(peers - 1):
            in_hop(index, step).wait_send()
    rim_copy.wait_send()
    cot_stay.wait()
    for number in range(tiles):
        tile_copy(number).wait()
    for copy in out_copies:
        copy.wait()
    if ring_out:
        for index in range(len(out_pieces)):
            for step in range(peers - 1):
                out_hop(index, step).wait_send()


SMALL_ROWS = 32


def gather_start(small, chunk, layer_input, cotangent, out_rows):
    peers, heads = lax.axis_size("shard"), lax.axis_size("head")
    tokens = layer_input.shape[0]
    chips = heads // 2
    piece_rows = out_rows.shape[0]
    ring_out = piece_rows % 32 == 0
    pieces = cut_rows(chunk.shape[0], 16)
    out_pieces = cut_rows(piece_rows, 16) if ring_out else []
    inside = pl.BlockSpec(memory_space=pltpu.VMEM)
    outside = pl.BlockSpec(memory_space=pl.ANY)
    sems = pltpu.SemaphoreType.DMA
    group, cols = heads * tokens, chunk.shape[1]
    full_out_shape = (peers * piece_rows, D)
    head_sems = [sems((chips - 1,)), sems((chips - 1,)), sems((chips,)), sems((chips,))]
    return pl.pallas_call(
        functools.partial(gather_kernel, ring_out, pieces, out_pieces),
        out_shape=[
            jax.ShapeDtypeStruct((D, cols), BF16),
            jax.ShapeDtypeStruct((group, D), BF16),
            jax.ShapeDtypeStruct((group, D), BF16),
            jax.ShapeDtypeStruct((group, cols), BF16),
            jax.ShapeDtypeStruct((peers,) + small.shape, BF16),
            jax.ShapeDtypeStruct((HALO, cols), BF16),
        ]
        + ([jax.ShapeDtypeStruct(full_out_shape, BF16)] if ring_out else []),
        in_specs=[inside] * 4 + [inside if ring_out else outside],
        out_specs=[outside] * 4 + [inside] * 2 + ([outside] if ring_out else []),
        scratch_shapes=[
            pltpu.VMEM((D, cols), BF16),
            pltpu.VMEM((group, D), BF16),
            pltpu.VMEM((tokens, D), BF16),
            pltpu.VMEM((group, cols), BF16),
            pltpu.VMEM((peers - 1,) + small.shape, BF16),
            pltpu.VMEM((HALO, D), BF16),
            sems((peers - 1,)),
            sems((peers - 1,)),
            sems((len(pieces), peers - 1)),
            sems((len(pieces), peers - 1)),
            *head_sems,
            *head_sems,
            sems(()),
            sems(()),
            sems((5,)),
            sems((group // BLOCK,)),
        ]
        + (
            [
                pltpu.VMEM(full_out_shape, BF16),
                sems(()),
                sems(()),
                sems((len(out_pieces), peers - 1)),
                sems((len(out_pieces), peers - 1)),
            ]
            if ring_out
            else []
        ),
        compiler_params=pltpu.CompilerParams(
            collective_id=0, has_side_effects=True, vmem_limit_bytes=60 * 1024 * 1024
        ),
        name="gather_start",
    )(small, chunk, layer_input, cotangent, out_rows)


def ring_stream(peers, place, following, preceding, grad, slots, rows, first, size, way, sends, recvs):
    def local(step):
        owner = ring_shard(place - way * (1 + step), peers)
        return grad.at[pl.ds(pl.multiple_of(owner * rows + first, 8), size)]

    def copy(step):
        return remote(
            local(0) if step == 0 else slots.at[step - 1],
            slots.at[step],
            sends.at[step],
            recvs.at[step],
            {"shard": following if way > 0 else preceding},
        )

    def send(step):
        if step:
            copy(step - 1).wait_recv()
            slots[step - 1] = slots[step - 1] + local(step)[...]
        copy(step).start()

    def finish(target):
        copy(peers - 2).wait_recv()
        target[pl.ds(first, size), :] = slots[peers - 2] + local(peers - 1)[...]

    def drain():
        for step in range(peers - 1):
            copy(step).wait_send()

    return send, finish, drain


class Fold:
    tile = 256

    def __init__(self, product, tokens, give, got, far_out, far_in, total, sems):
        self.product, self.tokens = product, tokens
        self.give, self.got, self.far_out, self.far_in, self.total = give, got, far_out, far_in, total
        self.near_send, self.near_recv, self.far_send, self.far_recv = sems
        peers = lax.axis_size("head")
        mine = lax.axis_index("head")
        self.chips = peers // 2
        self.chip, self.core = lax.div(mine, 2), lax.rem(mine, 2)
        self.sibling, self.there, _ = head_peers()

    def near(self, by):
        return remote(
            self.give, self.got.at[by], self.near_send.at[by], self.near_recv.at[by], {"head": self.sibling}
        )

    def far(self, by):
        return remote(
            self.far_out.at[by - 1], self.far_in.at[by - 1], self.far_send.at[by - 1], self.far_recv.at[by - 1],
            {"head": self.there[by - 1]},
        )

    def rows(self, by, core, write):
        owner = lax.rem(self.chip + by, self.chips) * 2 + core

        def step(i, carry):
            here = pl.multiple_of(i * self.tile, self.tile)
            write(pl.ds(here, self.tile), self.product(pl.multiple_of(owner * self.tokens + here, self.tile), self.tile))
            return carry

        lax.fori_loop(0, self.tokens // self.tile, step, 0)

    def tasks(self):
        order = list(range(1, self.chips)) + [0]
        tasks = []
        for number, by in enumerate(order):

            def hand(by=by, before=order[number - 1] if number else None):
                if before is not None:
                    self.near(before).wait_send()

                def write(at, value):
                    self.give[at, :] = value

                self.rows(by, 1 - self.core, write)
                self.near(by).start()

            tasks.append(hand)
        for by in order:

            def keep(by=by):
                self.near(by).wait_recv()

                def write(at, value):
                    value = value + self.got[by, at, :]
                    if by:
                        self.far_out[by - 1, at, :] = value.astype(BF16)
                    else:
                        self.total[at, :] = value

                self.rows(by, self.core, write)
                if by:
                    self.far(by).start()

            tasks.append(keep)
        return tasks

    def arrive(self):
        for by in range(1, self.chips):
            self.far(by).wait_recv()

    def whole(self, at):
        value = self.total[at, :]
        for by in range(1, self.chips):
            value = value + self.far_in[by - 1, at, :].astype(F32)
        return value

    def drain(self):
        self.near(0).wait_send()
        for by in range(1, self.chips):
            self.far(by).wait_send()


def fold_scratch(tokens):
    chips = lax.axis_size("head") // 2
    sems = pltpu.SemaphoreType.DMA
    return [
        pltpu.VMEM((tokens, D), F32),
        pltpu.VMEM((chips, tokens, D), F32),
        pltpu.VMEM((chips - 1, tokens, D), BF16),
        pltpu.VMEM((chips - 1, tokens, D), BF16),
        sems((chips,)),
        sems((chips,)),
        sems((chips - 1,)),
        sems((chips - 1,)),
    ]


def ring_chain_kernel(
    gate_pieces, out_pieces, gate_ref, out_ref, own_ref, decay_ref, mixed_ref, full_ref, input_ref,
    part_gate_ref, part_out_ref, after_ref, result_ref,
    gate_slots, out_slots, outbox, inbox, gate_send, gate_recv, out_send, out_recv, chain_send, chain_recv,
    give, got, far_out, far_in, near_sends, near_recvs, far_sends, far_recvs,
):
    peers = lax.axis_size("shard")
    shard = lax.axis_index("shard")
    sibling, there, _ = head_peers()
    place = ring_position(shard, peers)
    following, preceding = ring_shard(place + 1, peers), ring_shard(place - 1, peers)
    barrier = greet(
        [{"shard": following}, {"shard": preceding}, {"head": sibling}]
        + [{"head": other} for other in there]
    )

    @pl.when(shard < peers - 1)
    def _():
        pl.semaphore_signal(barrier, inc=1, device_id={"shard": shard + 1}, device_id_type=MESH)

    @pl.when(shard > 0)
    def _():
        pl.semaphore_wait(barrier, 4 + len(there))

    @pl.when(shard == 0)
    def _():
        pl.semaphore_wait(barrier, 3 + len(there))

    streams = []
    for cuts, grad, slots, part, sends, recvs in (
        (gate_pieces, gate_ref, gate_slots, part_gate_ref, gate_send, gate_recv),
        (out_pieces, out_ref, out_slots, part_out_ref, out_send, out_recv),
    ):
        for number, (first, size, way) in enumerate(cuts):
            stream = ring_stream(
                peers, place, following, preceding, grad, slots.at[number],
                part.shape[0], first, size, way, sends.at[number], recvs.at[number],
            )
            streams.append((*stream, part))

    def product(row, rows):
        return contract(mixed_ref[pl.ds(row, rows), :], full_ref[...], NN)

    fold = Fold(
        product, input_ref.shape[0], give, got, far_out, far_in, result_ref,
        (near_sends, near_recvs, far_sends, far_recvs),
    )
    tasks = fold.tasks()

    turn = peers - 1 - shard
    chain_copy = remote(outbox, inbox, chain_send, chain_recv, {"shard": lax.rem(shard + peers - 1, peers)})

    def chain_step(step):
        @pl.when(turn == step)
        def _():
            if step == 0:
                after_ref[...] = jnp.zeros_like(after_ref)
            else:
                chain_copy.wait_recv()
                after_ref[...] = inbox[...]
            if step < peers - 1:
                outbox[...] = after_ref[...] * decay_ref[0:1, :] + own_ref[...]
                chain_copy.start()

    for step in range(peers - 1):
        for send, _, _, _ in streams:
            send(step)
        chain_step(step)
        if step < len(tasks):
            tasks[step]()
    chain_step(peers - 1)
    for task in tasks[peers - 1 :]:
        task()
    for _, finish, _, part in streams:
        finish(part)
    fold.arrive()
    for start in range(0, input_ref.shape[0], Fold.tile):
        at = pl.ds(start, Fold.tile)
        result_ref[at, :] = input_ref[at, :] + fold.whole(at)
    fold.drain()
    for _, _, drain, _ in streams:
        drain()

    @pl.when(shard > 0)
    def _():
        chain_copy.wait_send()


def slots_of(pieces, peers, cols):
    sizes = {size for _, size, _ in pieces}
    return pltpu.VMEM((len(pieces), peers - 1, max(sizes), cols), F32)


def even_pieces(rows):
    pieces = cut_rows(rows, 8)
    if len({size for _, size, _ in pieces}) > 1:
        step = 8
        pieces = [
            (start, step, 1 if number % 2 == 0 else -1)
            for number, start in enumerate(range(0, rows, step))
        ]
    return pieces


def ring_chain(grad_gate, grad_out, own, decay, mixed, full_out, layer_input):
    peers = lax.axis_size("shard")
    gate_pieces = even_pieces(grad_gate.shape[0] // peers)
    out_pieces = even_pieces(grad_out.shape[0] // peers)
    inside = pl.BlockSpec(memory_space=pltpu.VMEM)
    sems = pltpu.SemaphoreType.DMA
    return pl.pallas_call(
        functools.partial(ring_chain_kernel, gate_pieces, out_pieces),
        out_shape=[
            jax.ShapeDtypeStruct((grad_gate.shape[0] // peers, grad_gate.shape[1]), F32),
            jax.ShapeDtypeStruct((grad_out.shape[0] // peers, grad_out.shape[1]), F32),
            jax.ShapeDtypeStruct(own.shape, F32),
            jax.ShapeDtypeStruct(layer_input.shape, F32),
        ],
        in_specs=[inside] * 7,
        out_specs=[inside] * 4,
        scratch_shapes=[
            slots_of(gate_pieces, peers, grad_gate.shape[1]),
            slots_of(out_pieces, peers, grad_out.shape[1]),
            pltpu.VMEM(own.shape, F32),
            pltpu.VMEM(own.shape, F32),
            sems((len(gate_pieces), peers - 1)),
            sems((len(gate_pieces), peers - 1)),
            sems((len(out_pieces), peers - 1)),
            sems((len(out_pieces), peers - 1)),
            sems(()),
            sems(()),
        ]
        + fold_scratch(layer_input.shape[0]),
        compiler_params=pltpu.CompilerParams(
            collective_id=2, has_side_effects=True, vmem_limit_bytes=60 * 1024 * 1024
        ),
        name="ring_gate_out",
    )(grad_gate, grad_out, own, decay, mixed, full_out, layer_input)


def ring_rest_kernel(
    pieces, grad_ref, gate_ref, rest_ref, full_ref, input_ref, cot_ref, gain_ref, small_ref,
    part_gate_ref, part_out_ref, all_ref, dinput_ref, small_out_ref, all_gate_ref, all_out_ref,
    slots, part, ring_send, ring_recv, out_send, out_recv, next_send, next_recv, local_sems,
    small_in, gain_mine, gain_in, small_all, small_send, small_recv, gain_send, gain_recv, all_send, all_recv,
    out_piece, piece_send, piece_recv, gate_sems, out_sems, stay_sems,
    give, got, far_out, far_in, near_sends, near_recvs, far_sends, far_recvs,
):
    peers, heads = lax.axis_size("shard"), lax.axis_size("head")
    shard, head = lax.axis_index("shard"), lax.axis_index("head")
    sibling, there, source = head_peers()
    place = ring_position(shard, peers)
    following, preceding = ring_shard(place + 1, peers), ring_shard(place - 1, peers)
    shards = [lax.rem(shard + by, peers) for by in range(1, peers)]
    mates = [lax.rem(head + by, heads) for by in range(1, heads)]
    barrier = greet([{"shard": other} for other in shards] + [{"head": other} for other in mates])
    stored_by, worked_by, at_home = home_of(head, shard, heads, peers)
    greet_across(barrier, worked_by, at_home, len(shards) + len(mates))
    piece_copy = remote(part_out_ref, out_piece, piece_send, piece_recv, stored_by)
    gate_gather = HeadGather(part_gate_ref, all_gate_ref, [gate_sems.at[i] for i in range(4)])
    out_gather = HeadGather(out_piece, all_out_ref, [out_sems.at[i] for i in range(4)])
    stays = [
        pltpu.make_async_copy(part_gate_ref, gate_gather.at(head), stay_sems.at[0]),
        pltpu.make_async_copy(out_piece, out_gather.at(head), stay_sems.at[1]),
    ]
    rows = part.shape[0]
    tokens = input_ref.shape[0]
    small_rows = small_ref.shape[1]
    streams = [
        ring_stream(
            peers, place, following, preceding, grad_ref, slots.at[number],
            rows, first, size, way, ring_send.at[number], ring_recv.at[number],
        )
        for number, (first, size, way) in enumerate(pieces)
    ]
    gate_width, rest_width = gate_ref.shape[1], rest_ref.shape[1]

    def product(row, count):
        at = pl.ds(row, count)
        return contract(gate_ref[at, :], full_ref[:, 0:gate_width], NT) + contract(
            rest_ref[at, :], full_ref[:, gate_width : gate_width + rest_width], NT
        )

    fold = Fold(
        product, tokens, give, got, far_out, far_in, dinput_ref,
        (near_sends, near_recvs, far_sends, far_recvs),
    )
    tasks = fold.tasks()
    small_copies = [
        remote(
            small_ref.at[shards[by]], small_in.at[by], small_send.at[by], small_recv.at[by], {"shard": shards[by]}
        )
        for by in range(peers - 1)
    ]
    for step in range(peers - 1):
        for send, _, _ in streams:
            send(step)
        if step == 0:
            for copy in small_copies:
                copy.start()

            @pl.when(jnp.logical_not(at_home))
            def _():
                piece_copy.start()

            @pl.when(at_home)
            def _():
                out_piece[...] = part_out_ref[...]

            gate_gather.start()
            stays[0].start()
        if step == 2:

            @pl.when(jnp.logical_not(at_home))
            def _():
                piece_copy.wait()

            gate_gather.pass_on()
            out_gather.start()
            stays[1].start()
        if step == 4:
            out_gather.pass_on()
        if step < len(tasks):
            tasks[step]()
    for task in tasks[peers - 1 :]:
        task()

    def at_rows(owner, first, size):
        return pl.ds(pl.multiple_of(owner * rows + first, 8), size)

    waits, far = [], []
    for number, (first, size, _) in enumerate(pieces):
        streams[number][1](part)
        mine = part.at[pl.ds(first, size)]
        target = all_ref.at[at_rows(head, first, size)]
        for by in range(len(there)):
            copy = remote(mine, target, out_send.at[number, by], out_recv.at[number, by], {"head": there[by]})
            copy.start()
            far.append((number, by, copy))
        copy = remote(mine, target, next_send.at[number, 0], next_recv.at[number, 0], {"head": sibling})
        copy.start()
        waits.append(copy)
        copy = pltpu.make_async_copy(mine, target, local_sems.at[number])
        copy.start()
        waits.append(copy)

    fold.arrive()
    gain = gain_ref[0:1, :]
    gain_sum = jnp.zeros((8, D), F32)
    for start in range(0, tokens, Fold.tile):
        at = pl.ds(start, Fold.tile)
        d_normed = fold.whole(at)
        value = input_ref[at, :]
        scale = lax.rsqrt(jnp.mean(value * value, axis=-1, keepdims=True) + EPSILON)
        unit = value * scale
        product_rows = d_normed * unit
        for group in range(0, Fold.tile, 8):
            gain_sum = gain_sum + product_rows[group : group + 8, :]
        d_hat = d_normed * gain
        dinput_ref[at, :] = cot_ref[at, :] + scale * (
            d_hat - unit * jnp.mean(d_hat * unit, axis=-1, keepdims=True)
        )
    gain_row = jnp.sum(gain_sum, axis=0, keepdims=True)
    gain_mine[...] = jnp.concatenate(
        [gain_row[:, start : start + LANES] for start in range(0, D, LANES)]
        + [jnp.zeros((16 - D // LANES, LANES), F32)],
        axis=0,
    )
    gain_copies = [
        remote(gain_mine, gain_in.at[by], gain_send.at[by], gain_recv.at[by], {"shard": shards[by]})
        for by in range(peers - 1)
    ]
    for copy in gain_copies:
        copy.start()
    for number, by, copy in far:
        first, size, _ = pieces[number]
        copy.wait_recv()
        landed = all_ref.at[at_rows(source[by], first, size)]
        onward = remote(
            landed, landed, next_send.at[number, 1 + by], next_recv.at[number, 1 + by], {"head": sibling}
        )
        onward.start()
        waits.append(onward)

    small = small_ref[pl.ds(shard, 1)][0]
    gains = gain_mine[...]
    for copy in small_copies + gain_copies:
        copy.wait_recv()
    for by in range(peers - 1):
        small = small + small_in[by]
        gains = gains + gain_in[by]
    small_all[pl.ds(head, 1), 0:small_rows, :] = small[None]
    small_all[pl.ds(head, 1), small_rows:, :] = gains[None]
    all_copies = [
        remote(
            small_all.at[head], small_all.at[head], all_send.at[by], all_recv.at[by], {"head": mates[by]}
        )
        for by in range(heads - 1)
    ]
    for copy in all_copies:
        copy.start()
    for copy in all_copies:
        copy.wait_recv()
    everything = small_all[0]
    for other in range(1, heads):
        everything = everything + small_all[other]
    small_out_ref[...] = everything

    for gather in (gate_gather, out_gather):
        gather.finish()
        gather.drain()
    for copy in waits + stays:
        copy.wait()
    for _, _, copy in far:
        copy.wait_send()
    for copy in small_copies + gain_copies + all_copies:
        copy.wait_send()
    fold.drain()
    for _, _, drain in streams:
        drain()


def ring_rest(grad, d_gate, d_rest, full_in, layer_input, cotangent, gain, small, part_gate, part_out):
    peers, heads = lax.axis_size("shard"), lax.axis_size("head")
    chips = heads // 2
    rows, cols = grad.shape[0] // peers, grad.shape[1]
    pieces = even_pieces(rows)
    count = len(pieces)
    small_rows = small.shape[1]
    sems = pltpu.SemaphoreType.DMA
    inside = pl.BlockSpec(memory_space=pltpu.VMEM)
    outside = pl.BlockSpec(memory_space=pl.ANY)
    return pl.pallas_call(
        functools.partial(ring_rest_kernel, pieces),
        out_shape=[
            jax.ShapeDtypeStruct((heads * rows, cols), F32),
            jax.ShapeDtypeStruct(layer_input.shape, F32),
            jax.ShapeDtypeStruct((small_rows + 16, LANES), F32),
            jax.ShapeDtypeStruct((heads * part_gate.shape[0], part_gate.shape[1]), F32),
            jax.ShapeDtypeStruct((heads * part_out.shape[0], part_out.shape[1]), F32),
        ],
        in_specs=[inside] * 10,
        out_specs=[outside, inside, inside, outside, outside],
        scratch_shapes=[
            slots_of(pieces, peers, cols),
            pltpu.VMEM((rows, cols), F32),
            sems((count, peers - 1)),
            sems((count, peers - 1)),
            sems((count, max(chips - 1, 1))),
            sems((count, max(chips - 1, 1))),
            sems((count, chips)),
            sems((count, chips)),
            sems((count,)),
            pltpu.VMEM((peers - 1, small_rows, LANES), F32),
            pltpu.VMEM((16, LANES), F32),
            pltpu.VMEM((peers - 1, 16, LANES), F32),
            pltpu.VMEM((heads, small_rows + 16, LANES), F32),
            sems((peers - 1,)),
            sems((peers - 1,)),
            sems((peers - 1,)),
            sems((peers - 1,)),
            sems((heads - 1,)),
            sems((heads - 1,)),
            pltpu.VMEM(part_out.shape, F32),
            sems(()),
            sems(()),
            sems((4, chips)),
            sems((4, chips)),
            sems((2,)),
        ]
        + fold_scratch(layer_input.shape[0]),
        compiler_params=pltpu.CompilerParams(
            collective_id=3, has_side_effects=True, vmem_limit_bytes=60 * 1024 * 1024
        ),
        name="ring_rest",
    )(grad, d_gate, d_rest, full_in, layer_input, cotangent, gain, small, part_gate, part_out)


def exchange_kernel(
    width, own_bc, rest_in_ref, bc_ref, first_ref, tail_ref, taps_ref, rest_ref,
    after, sent, got, apart, misc, edge, edge_send, edge_recv, near_send, near_recv, far_send, far_recv, local_sems,
):
    peers = lax.axis_size("shard")
    shard, head = lax.axis_index("shard"), lax.axis_index("head")
    sibling, there, _ = head_peers()
    chips = lax.axis_size("head") // 2
    chip, core = lax.div(head, 2), lax.rem(head, 2)
    tokens = bc_ref.shape[1]
    following, preceding = lax.rem(shard + 1, peers), lax.rem(shard + peers - 1, peers)
    barrier = greet(
        [{"shard": following}, {"head": sibling}] + [{"head": other} for other in there]
    )
    pl.semaphore_wait(barrier, 2 + len(there))
    edge_copy = remote(first_ref, after, edge_send, edge_recv, {"shard": preceding})
    edge_copy.start()
    read = pltpu.make_async_copy(rest_ref.at[:, pl.ds(width, LANES)], misc, local_sems.at[0])
    read.start()
    edge_copy.wait_recv()
    nearer = jnp.where(shard < peers - 1, 1.0, 0.0)
    reach_back = jnp.zeros((16, first_ref.shape[1]), F32)
    for tap in range(CONV - 1):
        reach = CONV - 1 - tap
        reach_back = reach_back + jnp.concatenate(
            [
                jnp.zeros((16 - reach, first_ref.shape[1]), F32),
                taps_ref[tap : tap + 1, :] * after[0:reach, :] * nearer,
            ],
            axis=0,
        )
    edge[...] = (tail_ref[:, 0:width] + reach_back[:, 0:width]).astype(BF16)
    write_edge = pltpu.make_async_copy(
        edge, rest_ref.at[pl.ds(tokens - 16, 16), pl.ds(0, width)], local_sems.at[1]
    )
    write_edge.start()
    last = slice(tokens - LANES, tokens)
    turned = [
        jnp.transpose(
            jnp.concatenate(
                [
                    jnp.zeros((LANES - 16, NSTATE), F32),
                    reach_back[:, width + part * NSTATE : width + (part + 1) * NSTATE],
                ],
                axis=0,
            )
        )
        for part in range(2)
    ]
    is_second = core == 1
    sent[...] = jnp.where(is_second, bc_ref[0:NSTATE, :], bc_ref[NSTATE:, :])
    sent[:, last] = sent[:, last] + jnp.where(is_second, turned[0], turned[1])
    near = remote(sent, got, near_send, near_recv, {"head": sibling})
    near.start()
    near.wait_recv()
    got[...] = got[...] + jnp.where(is_second, bc_ref[NSTATE:, :], bc_ref[0:NSTATE, :])
    got[:, last] = got[:, last] + jnp.where(is_second, turned[1], turned[0])
    far = []
    for by in range(1, chips):
        theirs = pl.ds(pl.multiple_of(lax.rem(chip + by, chips) * own_bc, 8), own_bc)
        far.append(
            remote(
                got.at[theirs], apart.at[by - 1], far_send.at[by - 1], far_recv.at[by - 1],
                {"head": there[by - 1]},
            )
        )
        far[-1].start()
    read.wait()
    for copy in far:
        copy.wait_recv()
    mine = pl.ds(pl.multiple_of(chip * own_bc, 8), own_bc)
    lane_id = lax.broadcasted_iota(jnp.int32, (BLOCK, LANES), 1)
    for start in range(0, tokens, BLOCK):
        cols = slice(start, start + BLOCK)
        share = got[mine, cols]
        for by in range(1, chips):
            share = share + apart[by - 1, :, cols]
        share = jnp.transpose(
            jnp.concatenate([share, jnp.zeros((LANES - own_bc, BLOCK), F32)], axis=0)
        )
        misc[cols, :] = jnp.where(lane_id < own_bc, share, misc[cols, :].astype(F32)).astype(BF16)
    write = pltpu.make_async_copy(misc, rest_ref.at[:, pl.ds(width, LANES)], local_sems.at[2])
    write.start()
    write.wait()
    write_edge.wait()
    edge_copy.wait_send()
    near.wait_send()
    for copy in far:
        copy.wait_send()


def exchange(d_rest, d_bc, first, tail, taps, width, own_bc):
    chips = lax.axis_size("head") // 2
    tokens = d_rest.shape[0]
    sems = pltpu.SemaphoreType.DMA
    inside = pl.BlockSpec(memory_space=pltpu.VMEM)
    outside = pl.BlockSpec(memory_space=pl.ANY)
    return pl.pallas_call(
        functools.partial(exchange_kernel, width, own_bc),
        out_shape=jax.ShapeDtypeStruct(d_rest.shape, d_rest.dtype),
        in_specs=[outside] + [inside] * 4,
        out_specs=outside,
        input_output_aliases={0: 0},
        scratch_shapes=[
            pltpu.VMEM(first.shape, F32),
            pltpu.VMEM((NSTATE, tokens), F32),
            pltpu.VMEM((NSTATE, tokens), F32),
            pltpu.VMEM((chips - 1, own_bc, tokens), F32),
            pltpu.VMEM((tokens, LANES), BF16),
            pltpu.VMEM((16, width), BF16),
            sems(()),
            sems(()),
            sems(()),
            sems(()),
            sems((chips - 1,)),
            sems((chips - 1,)),
            sems((3,)),
        ],
        compiler_params=pltpu.CompilerParams(
            collective_id=4, has_side_effects=True, vmem_limit_bytes=VMEM_LIMIT
        ),
        name="exchange",
    )(d_rest, d_bc, first, tail, taps)


UPDATE_ROWS = 24


def update_kernel(
    own_bc, local_heads, gate_ref, rest_ref, out_ref, win_ref, fin_ref, sin_ref, wout_ref, fout_ref, sout_ref,
    one_in_ref, two_in_ref, new_in_ref, one_out_ref, two_out_ref, new_out_ref,
):
    heads, _, width = gate_ref.shape

    def step(refs, cols, gradient):
        weight, first, second, one, two, new = refs
        one[:, cols], two[:, cols], new[:, cols] = adamw(
            weight[:, cols], first[:, cols], second[:, cols], gradient, RATE_MATRIX, DECAY_MATRIX
        )

    into = (win_ref, fin_ref, sin_ref, one_in_ref, two_in_ref, new_in_ref)
    for head in range(heads):
        step(into, slice(head * width, (head + 1) * width), gate_ref[head])
        step(into, slice(DI + head * width, DI + (head + 1) * width), rest_ref[head, :, 0:width])
    order = [chip * 2 + core for core in range(2) for chip in range(heads // 2)]
    tail = [rest_ref[head, :, width : width + own_bc] for head in order] + [
        rest_ref[head, :, width + own_bc : width + own_bc + local_heads] for head in range(heads)
    ]
    step(into, slice(2 * DI, 2 * DI + 2 * NSTATE + HEADS), jnp.concatenate(tail, axis=1))
    out = (wout_ref, fout_ref, sout_ref, one_out_ref, two_out_ref, new_out_ref)
    step(out, slice(0, D), out_ref[...])


def update(all_gate, all_rest, all_out, into, out, own_bc, local_heads):
    heads = lax.axis_size("head")
    rows, cols = into[0].shape
    steps = rows // UPDATE_ROWS
    out_rows = out[0].shape[0] // steps
    whole = lambda i: (0, i, 0)
    flat = lambda i: (i, 0)
    all_gate = all_gate.reshape(heads, rows, -1)
    all_rest = all_rest.reshape(heads, rows, -1)
    in_block, out_block = (UPDATE_ROWS, cols), (out_rows, D)
    return blocked(
        functools.partial(update_kernel, own_bc, local_heads),
        "update",
        steps,
        [
            (all_gate, (heads, UPDATE_ROWS, all_gate.shape[2]), whole),
            (all_rest, (heads, UPDATE_ROWS, all_rest.shape[2]), whole),
            (all_out, out_block, flat),
        ]
        + [(array, in_block, flat) for array in into]
        + [(array, out_block, flat) for array in out],
        [(into[0].shape, F32, in_block, flat)] * 3 + [(out[0].shape, F32, out_block, flat)] * 3,
        [],
        10**8,
        5 * 10**7,
    )


def row_owner_pairs(head_count, shard_count):
    pairs = []
    for stored in range(shard_count):
        for slot in range(head_count):
            piece = stored * head_count + slot
            head, shard = piece // shard_count, piece % shard_count
            pairs.append((slot * shard_count + stored, head * shard_count + shard))
    return pairs


def per_device(
    layer_input,
    cotangent,
    weight_in,
    first_in,
    second_in,
    weight_out,
    first_out,
    second_out,
    small_params,
    first_small,
    second_small,
):
    head_count = lax.axis_size("head")
    shard_count = lax.axis_size("shard")
    tok_rows = layer_input.shape[0]
    group_rows = head_count * tok_rows
    local_heads = HEADS // head_count
    head_width = DI // head_count
    block_count = group_rows // BLOCK
    own_bc = 2 * NSTATE // head_count
    head_index = lax.axis_index("head")
    shard_index = lax.axis_index("shard")
    chip_index, core_index = head_index // 2, head_index % 2
    chan_start = head_index * head_width
    head_start = head_index * local_heads
    bc_start = core_index * NSTATE + chip_index * own_bc

    misc = LANES
    columns = [
        lax.dynamic_slice_in_dim(weight_in, chan_start, head_width, 1),
        lax.dynamic_slice_in_dim(weight_in, DI + chan_start, head_width, 1),
        lax.dynamic_slice_in_dim(weight_in, 2 * DI + bc_start, own_bc, 1),
        lax.dynamic_slice_in_dim(weight_in, DI + XBC + head_start, local_heads, 1),
        jnp.zeros((weight_in.shape[0], misc - own_bc - local_heads), F32),
        weight_in[:, 2 * DI : DI + XBC],
    ]
    at_x, at_misc, at_bc = head_width, 2 * head_width, 2 * head_width + misc
    at_dt = at_misc + own_bc
    small_low = small_params.astype(BF16)
    own_small = small_low.shape[0]
    flat = lax.dynamic_update_slice_in_dim(
        jnp.zeros((own_small * shard_count,), BF16), small_low, shard_index * own_small, 0
    )
    small_block = jnp.concatenate(
        [
            jnp.pad(small_low, (0, SMALL_ROWS * LANES - own_small)).reshape(SMALL_ROWS, LANES),
            jnp.pad(flat[-D:].reshape(D // LANES, LANES), ((0, 16 - D // LANES), (0, 0))),
        ],
        axis=0,
    )
    piece_rows = weight_out.shape[0] // head_count
    chunk = jnp.concatenate(columns, axis=1).astype(BF16)
    out_piece = lax.dynamic_slice_in_dim(weight_out, head_index * piece_rows, piece_rows, 0).astype(BF16)
    full_in, normed, cot_low, projected, smalls, before, *full_out = gather_start(
        small_block, chunk, layer_input, cotangent, out_piece
    )
    if full_out:
        (full_out,) = full_out
    else:
        pairs = row_owner_pairs(head_count, shard_count)
        out_piece = lax.ppermute(out_piece, ("head", "shard"), pairs)
        full_out = lax.all_gather(out_piece, "shard", axis=0, tiled=True)
    full_small = smalls[:, :SMALL_ROWS].reshape(shard_count, -1)[:, :own_small].reshape(-1)
    conv_weight, conv_bias, dt_bias, a_log, skip_all, norm_all, pre_gain = unpack(
        full_small.astype(F32)
    )
    d_mixed = jnp.einsum("td,id->ti", cot_low, full_out, preferred_element_type=F32)

    width, span = head_width, head_width + 2 * NSTATE
    taps = jnp.concatenate(
        [
            jnp.concatenate(
                [lax.dynamic_slice_in_dim(conv_weight, chan_start, width, 1), conv_weight[:, DI:]], 1
            ),
            jnp.concatenate(
                [lax.dynamic_slice_in_dim(conv_bias, chan_start, width, 0), conv_bias[DI:]]
            )[None],
            jnp.zeros((8 - CONV - 1, span), F32),
        ],
        axis=0,
    )
    decay_rate = -jnp.exp(lax.dynamic_slice_in_dim(a_log, head_start, local_heads))
    offset_heads = lax.dynamic_slice_in_dim(dt_bias, head_start, local_heads)
    skip_gain = lax.dynamic_slice_in_dim(skip_all, head_start, local_heads)
    norm_gain = lax.dynamic_slice_in_dim(norm_all, chan_start, width, 0)
    lanes = (own_bc, LANES - own_bc - local_heads)
    heads = jnp.pad(jnp.stack([offset_heads, decay_rate]), ((0, 6), lanes))
    chans = jnp.pad(jnp.stack([jnp.repeat(skip_gain, HEADDIM), norm_gain]), ((0, 6), (0, 0)))

    steps = block_count
    at_b = at_bc // LANES
    misc_at = at_misc // LANES
    ahead = lambda col: (lambda i: (i, col))
    back = lambda col: (lambda i: (steps - 1 - i, col))
    fixed = lambda col: (lambda i: (0, col))
    last_rows = lambda col: (lambda i: (jnp.maximum((steps - 1 - i) * (BLOCK // 16) - 1, 0), col))
    rows = (BLOCK, width)
    lane_rows = (BLOCK, LANES)
    halo_in = [
        (before, (16, width), fixed(1)),
        (before, (16, LANES), fixed(at_b)),
        (before, (16, LANES), fixed(at_b + 1)),
    ]
    act, der, times, own_state, own_decay = blocked(
        functools.partial(prepare_kernel, own_bc),
        "conv_states",
        steps,
        [
            (projected, rows, ahead(1)),
            (projected, lane_rows, ahead(at_b)),
            (projected, lane_rows, ahead(at_b + 1)),
            (projected, lane_rows, ahead(misc_at)),
            *halo_in,
            (taps, (8, span), fixed(0)),
            (heads, (8, LANES), fixed(0)),
        ],
        [
            ((group_rows, span), F32, (BLOCK, span), ahead(0)),
            ((group_rows, span), F32, (BLOCK, span), ahead(0)),
            ((group_rows, 2 * LANES), F32, (BLOCK, 2 * LANES), ahead(0)),
            ((NSTATE, width), F32, (NSTATE, width), fixed(0)),
            ((8, width), F32, (8, width), fixed(0)),
        ],
        [pltpu.VMEM((BLOCK + 8, span), F32), pltpu.VMEM((8, LANES), F32)],
        10**10,
        4 * 10**7,
    )
    prior = chain(own_state, own_decay, 1)
    y_mix, y_ssm, sums, states, final = blocked(
        functools.partial(forward_kernel, own_bc),
        "scan_forward",
        steps,
        [
            (act, (BLOCK, span), ahead(0)),
            (times, (BLOCK, 2 * LANES), ahead(0)),
            (projected, rows, ahead(0)),
            (d_mixed, rows, ahead(0)),
            (chans, (8, width), fixed(0)),
            (prior, (NSTATE, width), fixed(0)),
        ],
        [
            ((group_rows, width), BF16, rows, ahead(0)),
            ((group_rows, width), F32, rows, ahead(0)),
            ((8, group_rows), F32, (8, BLOCK), lambda i: (0, i)),
            ((steps * NSTATE, width), F32, (NSTATE, width), ahead(0)),
            ((NSTATE, width), F32, (NSTATE, width), fixed(0)),
        ],
        [],
        2 * 10**10,
        5 * 10**7,
    )
    sums = sum_head(sums)
    mixed, d_gate, d_y, own_grad, gain_rows = blocked(
        functools.partial(gate_kernel, own_bc),
        "gated_norm",
        steps,
        [
            (act, lane_rows, back(span // LANES - 1)),
            (times, lane_rows, back(1)),
            (projected, rows, back(0)),
            (d_mixed, rows, back(0)),
            (y_mix, rows, back(0)),
            (sums, (8, BLOCK), lambda i: (0, steps - 1 - i)),
            (chans, (8, width), fixed(0)),
        ],
        [
            ((group_rows, width), BF16, rows, back(0)),
            ((group_rows, width), BF16, rows, back(0)),
            ((group_rows, width), F32, rows, back(0)),
            ((NSTATE, width), F32, (NSTATE, width), fixed(0)),
            ((8, width), F32, (8, width), fixed(0)),
        ],
        [],
        10**10,
        5 * 10**7,
    )
    grad_norm_gain = gain_rows[0]
    grad_out = jnp.einsum("ti,td->id", mixed, cot_low, preferred_element_type=F32)
    grad_gate = jnp.einsum("td,tf->df", normed, d_gate, preferred_element_type=F32)
    part_gate, part_out, after, result = ring_chain(
        grad_gate, grad_out, own_grad, own_decay, mixed, full_out, layer_input
    )
    d_rest, d_bc, first_conv, rest_raw, grad_taps, skip_rows, head_rows = blocked(
        functools.partial(backward_kernel, own_bc, local_heads),
        "scan_backward",
        steps,
        [
            (act, (BLOCK, span), back(0)),
            (der, (BLOCK, span), back(0)),
            (times, (BLOCK, 2 * LANES), back(0)),
            (d_y, rows, back(0)),
            (y_ssm, rows, back(0)),
            (states, (NSTATE, width), back(0)),
            (final, (NSTATE, width), fixed(0)),
            (after, (NSTATE, width), fixed(0)),
            (projected, lane_rows, back(misc_at)),
            (projected, rows, back(1)),
            (projected, lane_rows, back(at_b)),
            (projected, lane_rows, back(at_b + 1)),
            (projected, (16, width), last_rows(1)),
            (projected, (16, LANES), last_rows(at_b)),
            (projected, (16, LANES), last_rows(at_b + 1)),
            *halo_in,
            (taps, (8, span), fixed(0)),
            (heads, (8, LANES), fixed(0)),
            (chans, (8, width), fixed(0)),
        ],
        [
            ((group_rows, width + LANES), BF16, (BLOCK, width + LANES), back(0)),
            ((2 * NSTATE, group_rows), F32, (2 * NSTATE, BLOCK), lambda i: (0, steps - 1 - i)),
            ((8, span), F32, (8, span), fixed(0)),
            ((16, span), F32, (16, span), fixed(0)),
            ((8, span), F32, (8, span), fixed(0)),
            ((8, width), F32, (8, width), fixed(0)),
            ((8, LANES), F32, (8, LANES), fixed(0)),
        ],
        [
            pltpu.VMEM((NSTATE, width), F32),
            pltpu.VMEM((8, LANES), F32),
            pltpu.VMEM((BLOCK + 8, span), F32),
            pltpu.VMEM((BLOCK + 8, span), F32),
            pltpu.VMEM((BLOCK, width), F32),
        ],
        5 * 10**10,
        6 * 10**7,
    )
    grad_convw, grad_convb = grad_taps[:CONV], grad_taps[CONV]
    grad_skip = jnp.sum(skip_rows[0].reshape(local_heads, HEADDIM), axis=1)
    grad_dtb = head_rows[0, own_bc : own_bc + local_heads]
    grad_alog = head_rows[1, own_bc : own_bc + local_heads] * decay_rate

    d_rest = exchange(d_rest, d_bc, first_conv, rest_raw, taps, width, own_bc)
    grad_rest = jnp.einsum("td,tf->df", normed, d_rest, preferred_element_type=F32)

    def place(values, start, width):
        zeros = jnp.zeros(values.shape[:-1] + (width,), F32)
        return lax.dynamic_update_slice_in_dim(zeros, values, start, values.ndim - 1)

    conv_w_full = jnp.concatenate(
        [place(grad_convw[:, :head_width], chan_start, DI), grad_convw[:, head_width:]], axis=1
    ).reshape(-1)
    conv_b_full = jnp.concatenate(
        [place(grad_convb[:head_width], chan_start, DI), grad_convb[head_width:]]
    )
    grad_small = jnp.concatenate(
        [
            conv_w_full,
            conv_b_full,
            place(grad_dtb, head_start, HEADS),
            place(grad_alog, head_start, HEADS),
            place(grad_skip, head_start, HEADS),
            place(grad_norm_gain, chan_start, DI),
            jnp.zeros((D,), F32),
        ]
    )
    small_rows = 8 * (-(-own_small // (8 * LANES)))
    small_out = jnp.pad(
        grad_small.reshape(shard_count, own_small), ((0, 0), (0, small_rows * LANES - own_small))
    ).reshape(shard_count, small_rows, LANES)
    gain_in = jnp.broadcast_to(pre_gain, (8, D))
    all_rest, d_input, small_sums, all_gate, all_out = ring_rest(
        grad_rest, d_gate, d_rest, full_in, layer_input, cotangent, gain_in, small_out,
        part_gate, part_out,
    )
    gain_flat = jnp.concatenate(
        [
            jnp.zeros((own_small * shard_count - D,), F32),
            small_sums[small_rows : small_rows + D // LANES].reshape(D),
        ]
    )
    total_small = small_sums[:small_rows].reshape(-1)[:own_small] + lax.dynamic_slice_in_dim(
        gain_flat, shard_index * own_small, own_small
    )

    one_in, two_in, new_in, one_out, two_out, new_out = update(
        all_gate, all_rest, all_out,
        (weight_in, first_in, second_in), (weight_out, first_out, second_out),
        own_bc, local_heads,
    )
    one_small, two_small, new_small = adamw(
        small_params, first_small, second_small, total_small, RATE_SMALL, 0.0
    )
    return (
        result,
        d_input,
        one_in,
        two_in,
        new_in,
        one_out,
        two_out,
        new_out,
        one_small,
        two_small,
        new_small,
    )


def solution(mesh):
    rows = P(("shard", "head"), None)
    owned = P("shard", None)
    packed = P("shard")
    return jax.shard_map(
        per_device,
        mesh=mesh,
        in_specs=(rows, rows) + (owned,) * 6 + (packed,) * 3,
        out_specs=(rows, rows) + (owned,) * 6 + (packed,) * 3,
        check_vma=False,
    )
```
